256 devices in a mesh: curve: 128 (over x, z, y_hi, core), sub: 2 (over y_lo).
Axes of the slice: x: 4, y: 4 (y_hi: 2, y_lo: 2; y = y_hi * 2 + y_lo), z: 8, core: 2. Of those that a mesh axis runs over, the one named last changes fastest.
Arguments:
- features: bfloat16 [131072, 512], P(('curve', 'sub')), may hold values from -6 to 6
- hub_features: bfloat16 [1024, 512], P(('curve', 'sub')), may hold values from -6 to 6
- hub_order: int32 [1024], replicated, may hold values from 0 to 1023, each once
- tile_values: bfloat16 [16384, 128, 128], P(('curve', 'sub')), may hold values from -0.1875 to 0.1875
- tile_dest: int32 [256, 64], P(('curve', 'sub')), may hold values from 0 to 3
- tile_source: int32 [256, 64], P(('curve', 'sub')), may hold values from 0 to 31, as said below
- tile_count: int32 [256], P(('curve', 'sub')), may hold values from 8 to 64, as said below
- self_weight: bfloat16 [512, 512], replicated, may hold values from -0.25 to 0.25
- neighbour_weight: bfloat16 [512, 512], replicated, may hold values from -0.25 to 0.25
- cotangent: bfloat16 [131072, 512], P(('curve', 'sub')), may hold values from -6 to 6
Outputs:
- embedding: bfloat16 [131072, 512], P(('curve', 'sub'))
- feature_gradient: float32 [131072, 512], P(('curve', 'sub'))
- hub_gradient: float32 [1024, 512], P(('curve', 'sub'))
- self_gradient: float32 [512, 512], replicated
- neighbour_gradient: float32 [512, 512], replicated
The draws below stay inside these ranges and needn't reach their ends.
Inputs may be any that keep to these rules, and one draw needn't show every extreme that they name: The first tile_count[p] slots of device p are live, the rest are unused; some device has all 64 slots live. `tile_source`: slot k of every device takes its source from the next region when k % 4 == 0, the previous region when k % 4 == 1, the own region when k % 4 == 2, and a hub block when k % 4 == 3.
All inputs are finite; a program needn't handle non-finite values.
Results may differ from the reference program's by a relative error of at most 0.0075.
Values may be sent and summed in bfloat16 or wider, within the bound.
No kernel may reach another device: no remote copies, remote signals or barrier semaphores. Data moves between devices by JAX's collectives and lax.ppermute only.
A program may use at most 128 MiB of HBM per device.

```python
import jax
import jax.numpy as jnp
from jax import lax

H = 512
BLK_DEV = 4
SLOTS = 64
HUBS = 1024
NODES = 131072
N_CURVE = 128
DEVICES = 256


def draw_tile_count(key, part):
    key = jax.random.fold_in(key, 11)
    first_key, second_key = jax.random.split(key)
    shifts = jax.random.randint(first_key, (DEVICES,), 0, 4)
    counts = SLOTS // jnp.left_shift(jnp.ones((DEVICES,), jnp.int32), shifts)
    counts = jnp.maximum(counts, 4)
    busiest = jax.random.randint(second_key, (), 0, DEVICES)
    return jnp.where(jnp.arange(DEVICES) == busiest, SLOTS, counts).astype(jnp.int32)


def draw_tile_source(key, part):
    key = jax.random.fold_in(key, 23)
    category = jnp.arange(SLOTS, dtype=jnp.int32) % 4
    lowest = jnp.array([4 * BLK_DEV, 0, 2 * BLK_DEV, 6 * BLK_DEV], jnp.int32)[category]
    spread = jnp.array([2 * BLK_DEV, 2 * BLK_DEV, 2 * BLK_DEV, HUBS // 128], jnp.int32)[category]
    raw = jax.random.randint(key, (DEVICES, SLOTS), 0, 1048576)
    return (lowest[None, :] + raw % spread[None, :]).astype(jnp.int32)


def with_ends(values, own_key, low, high):
    spot = [jax.random.randint(jax.random.fold_in(own_key, axis), (), 0, length) for axis, length in enumerate(values.shape)]
    widest = values.shape.index(max(values.shape))
    beside = spot[:widest] + [(spot[widest] + 1) % values.shape[widest]] + spot[widest + 1:]
    return values.at[tuple(spot)].set(low).at[tuple(beside)].set(high)


def block_levels(key, extent, pieces, low, top_value):
    def one(position, shards_of):
        draws = jax.random.uniform(jax.random.fold_in(jax.random.fold_in(key, 6), position), (shards_of,), jnp.float32, low / len(pieces), top_value / len(pieces))
        return jnp.repeat(jnp.exp(draws), extent[position] // shards_of).reshape((-1,) + (1,) * (len(extent) - position - 1))

    gain = one(*pieces[0])
    for cut in pieces[1:]:
        gain = gain * one(*cut)
    return gain


def bell_draw(key, extent, width, limit, shards=(), kind=jnp.bfloat16):
    result = jax.random.normal(key, extent, jnp.float32) * width
    if len(shards) > 0:
        result = block_levels(key, extent, shards, -0.22, 0.18) * result
    return jnp.clip(result, min=-limit, max=limit).astype(kind)


def setup_inputs(seed: int = 0) -> dict:
    keys = jax.random.split(jax.random.key(seed), 11)
    features = bell_draw(keys[0], (NODES, H), 1.0, 6.0, ((0, 256),))
    hub_features = bell_draw(keys[1], (HUBS, H), 1.0, 6.0, ((0, 256),))
    hub_order = jax.random.permutation(keys[2], HUBS).astype(jnp.int32)
    tile_values = bell_draw(keys[3], (DEVICES * SLOTS, 128, 128), (128 * SLOTS // (2 * BLK_DEV)) ** -0.5, 0.1875, ((0, 256),))
    tile_dest = with_ends(jax.random.randint(keys[4], (DEVICES, SLOTS), 0, BLK_DEV), jax.random.fold_in(keys[4], 1), 0, BLK_DEV - 1).astype(jnp.int32)
    tile_source = draw_tile_source(jax.random.fold_in(keys[10], 71), 0)
    tile_count = draw_tile_count(jax.random.fold_in(keys[10], 71), 0)
    self_weight = bell_draw(keys[7], (H, H), H ** -0.5, 0.25)
    neighbour_weight = bell_draw(keys[8], (H, H), H ** -0.5, 0.25)
    cotangent = bell_draw(keys[9], (NODES, H), 1.0, 6.0, ((0, 256),))
    return dict(features=features, hub_features=hub_features, hub_order=hub_order, tile_values=tile_values, tile_dest=tile_dest, tile_source=tile_source, tile_count=tile_count, self_weight=self_weight, neighbour_weight=neighbour_weight, cotangent=cotangent)


def silu_slope(pre_act):
    sigmoid_value = jax.nn.sigmoid(pre_act)
    return sigmoid_value * (1.0 + pre_act * (1.0 - sigmoid_value))


def reference(features, hub_features, hub_order, tile_values, tile_dest, tile_source, tile_count, self_weight, neighbour_weight, cotangent):
    local_rows = BLK_DEV * 128
    regions = features.reshape(N_CURVE, 2 * local_rows, H)
    zero_region = jnp.zeros((1, 2 * local_rows, H), features.dtype)
    padded = jnp.concatenate([zero_region, regions, zero_region], 0)
    hub_table = hub_features[hub_order]
    window_blocks = 6 * BLK_DEV
    table_blocks = window_blocks + HUBS // 128

    def scan_step(carry, device_index):
        grad_pad, hub_accum, self_accum, neigh_accum = carry
        region_index = device_index // 2
        window = lax.dynamic_slice_in_dim(padded, region_index, 3, 0).reshape(6 * local_rows, H)
        table = jnp.concatenate([window, hub_table], 0).reshape(table_blocks, 128, H)
        own_rows = lax.dynamic_slice_in_dim(features, device_index * local_rows, local_rows, 0)
        own_cot = lax.dynamic_slice_in_dim(cotangent, device_index * local_rows, local_rows, 0)
        values = lax.dynamic_slice_in_dim(tile_values, device_index * SLOTS, SLOTS, 0)
        dest_ids = tile_dest[device_index]
        source_ids = tile_source[device_index]
        live_count = tile_count[device_index]

        def forward_add(slot_index, aggregate):
            product = jnp.dot(values[slot_index], table[source_ids[slot_index]], preferred_element_type=jnp.float32)
            return aggregate.at[dest_ids[slot_index]].add(product)

        aggregate = lax.fori_loop(0, live_count, forward_add, jnp.zeros((BLK_DEV, 128, H), jnp.float32))
        neighbours = aggregate.reshape(local_rows, H).astype(jnp.bfloat16)
        pre_act = jnp.dot(own_rows, self_weight, preferred_element_type=jnp.float32) + jnp.dot(neighbours, neighbour_weight, preferred_element_type=jnp.float32)
        embedding = jax.nn.silu(pre_act).astype(jnp.bfloat16)
        slope_grad = (own_cot.astype(jnp.float32) * silu_slope(pre_act)).astype(jnp.bfloat16)
        self_part = lax.dot_general(own_rows, slope_grad, (((0,), (0,)), ((), ())), preferred_element_type=jnp.float32)
        neigh_part = lax.dot_general(neighbours, slope_grad, (((0,), (0,)), ((), ())), preferred_element_type=jnp.float32)
        back_neigh = lax.dot_general(slope_grad, neighbour_weight, (((1,), (1,)), ((), ())), preferred_element_type=jnp.float32).astype(jnp.bfloat16).reshape(BLK_DEV, 128, H)
        self_term = lax.dot_general(slope_grad, self_weight, (((1,), (1,)), ((), ())), preferred_element_type=jnp.float32)

        def backward_add(slot_index, table_grad):
            product = lax.dot_general(values[slot_index], back_neigh[dest_ids[slot_index]], (((0,), (0,)), ((), ())), preferred_element_type=jnp.float32)
            return table_grad.at[source_ids[slot_index]].add(product)

        table_grad = lax.fori_loop(0, live_count, backward_add, jnp.zeros((table_blocks, 128, H), jnp.float32))
        window_grad = table_grad[:window_blocks].reshape(3, 2 * local_rows, H)
        current = lax.dynamic_slice_in_dim(grad_pad, region_index, 3, 0)
        grad_pad = lax.dynamic_update_slice_in_dim(grad_pad, current + window_grad, region_index, 0)
        hub_accum = hub_accum + table_grad[window_blocks:].reshape(HUBS, H)
        return (grad_pad, hub_accum, self_accum + self_part, neigh_accum + neigh_part), (embedding, self_term)

    start = (jnp.zeros((N_CURVE + 2, 2 * local_rows, H), jnp.float32), jnp.zeros((HUBS, H), jnp.float32), jnp.zeros((H, H), jnp.float32), jnp.zeros((H, H), jnp.float32))
    final, stacked = lax.scan(scan_step, start, jnp.arange(DEVICES, dtype=jnp.int32))
    grad_pad, hub_accum, self_gradient, neighbour_gradient = final
    embedding = stacked[0].reshape(NODES, H)
    feature_gradient = grad_pad[1:-1].reshape(NODES, H) + stacked[1].reshape(NODES, H)
    hub_gradient = jnp.zeros((HUBS, H), jnp.float32).at[hub_order].set(hub_accum)
    return embedding, feature_gradient, hub_gradient, self_gradient, neighbour_gradient
```

```python
import functools

import jax
import jax.numpy as jnp
from jax import lax
from jax.experimental import pallas as pl
from jax.experimental.pallas import tpu as pltpu
from jax.sharding import Mesh
from jax.sharding import PartitionSpec as P

BF = jnp.bfloat16
F32 = jnp.float32
BLK = 128
AXES = ("x", "z", "yh", "core", "yl")
EXTENT = (4, 8, 2, 2, 2)
WIDE = ("z", "yh", "yl")
NEAR = ("x", "core")
N_WIDE, N_NEAR = 32, 8
REGIONS = 128


def to_region(value, by, flip):
    pairs = [
        (2 * c + s, 2 * (c + by) + (s ^ flip))
        for c in range(REGIONS)
        if 0 <= c + by < REGIONS
        for s in range(2)
    ]
    return lax.ppermute(value, AXES, pairs)


OTHERS = ((-1, 0), (-1, 1), (0, 1), (1, 0), (1, 1))


def spread(value, axes, count):
    copies = jnp.broadcast_to(value[None], (count,) + value.shape)
    return lax.all_to_all(copies, axes, 0, 0, tiled=True).reshape(-1, value.shape[-1])


def collect(value, axes):
    return lax.all_to_all(value, axes, 0, 0, tiled=True).astype(F32).sum(0)


def hub_of(position):
    low = position & 7
    core = (position >> 7) & 1
    mid = (position >> 3) & 15
    high = position >> 8
    return low | (core << 3) | (mid << 4) | (high << 8)


def dot(a, b, ca=1, cb=0):
    return lax.dot_general(a, b, (((ca,), (cb,)), ((), ())), preferred_element_type=F32)


def kernel(
    dest, source, count, side,
    features, prev_same, prev_other, own_other, next_same, next_other,
    hubs, order_col, order_row, tiles, self_weight, neigh_weight, cotangent,
    embedding, own_grad, g_prev_same, g_prev_other, g_own_other, g_next_same, g_next_other, reduced,
    table, sums, grads, neigh, slope, back, hub_grads, sems,
):
    live = count[0]
    flip = 4 * side[0]
    copies = []
    for n, (ref, cat, half) in enumerate((
        (next_same, 0, 0), (next_other, 0, 1), (prev_same, 1, 0),
        (prev_other, 1, 1), (features, 2, 0), (own_other, 2, 1),
    )):
        copy = pltpu.make_async_copy(ref, table.at[cat, pl.ds(half * 4 * BLK, 4 * BLK)], sems.at[n])
        copy.start()
        copies.append(copy)
    ids = hub_of(lax.broadcasted_iota(jnp.int32, (BLK, 1024), 1))
    for j in range(8):
        rows = pl.ds(j * BLK, BLK)
        pick = (order_col[rows, :] == ids).astype(F32).astype(BF)
        table[3, rows, :] = dot(pick, hubs[...]).astype(BF)
    sums[...] = jnp.zeros_like(sums)
    grads[...] = jnp.zeros_like(grads)
    for copy in copies:
        copy.wait()

    low = (16, 0, 8, 24)

    def slot(m, cat):
        k = 4 * m + cat
        block = source[0, k] - low[cat]
        if cat < 3:
            block = block ^ flip
        mask = jnp.where(k < live, 1.0, 0.0).astype(BF)
        return k, dest[0, k], pl.ds(pl.multiple_of(block * BLK, BLK), BLK), mask

    def forward(m, carry):
        for cat in range(4):
            k, d, rows, mask = slot(m, cat)
            sums[cat, d] += dot(tiles[k] * mask, table[cat, rows, :])
        return carry

    chunks = (live + 3) // 4
    lax.fori_loop(0, chunks, forward, 0)

    for b in range(4):
        rows = pl.ds(b * BLK, BLK)
        near = (sums[0, b] + sums[1, b] + sums[2, b] + sums[3, b]).astype(BF)
        neigh[rows, :] = near
        pre = dot(table[2, rows, :], self_weight[...]) + dot(near, neigh_weight[...])
        sig = jax.nn.sigmoid(pre)
        embedding[rows, :] = (pre * sig).astype(BF)
        grad = (cotangent[rows, :].astype(F32) * (sig * (1.0 + pre * (1.0 - sig)))).astype(BF)
        slope[rows, :] = grad
        back[rows, :] = dot(grad, neigh_weight[...], 1, 1).astype(BF)
        own_grad[rows, :] = dot(grad, self_weight[...], 1, 1)
    for i in range(4):
        columns = pl.ds(i * BLK, BLK)
        reduced[i, pl.ds(BLK, BLK), :] = dot(table[2, pl.ds(0, 4 * BLK), columns], slope[...], 0, 0).astype(BF)
        reduced[4 + i, pl.ds(BLK, BLK), :] = dot(neigh[:, columns], slope[...], 0, 0).astype(BF)

    def backward(m, carry):
        for cat in range(4):
            k, d, rows, mask = slot(m, cat)
            there = pl.ds(pl.multiple_of(d * BLK, BLK), BLK)
            grads[cat, rows, :] += dot(tiles[k] * mask, back[there, :], 0, 0)
        return carry

    lax.fori_loop(0, chunks, backward, 0)
    half, rest = pl.ds(0, 4 * BLK), pl.ds(4 * BLK, 4 * BLK)
    g_next_same[...] = grads[0, half, :].astype(BF)
    g_next_other[...] = grads[0, rest, :].astype(BF)
    g_prev_same[...] = grads[1, half, :].astype(BF)
    g_prev_other[...] = grads[1, rest, :].astype(BF)
    g_own_other[...] = grads[2, rest, :].astype(BF)
    own_grad[...] += grads[2, half, :]
    hub_grads[...] = grads[3].astype(BF)
    for i in range(8):
        ids = hub_of(lax.broadcasted_iota(jnp.int32, (BLK, 1024), 0) + i * BLK)
        place = (ids == order_row[...]).astype(F32).astype(BF)
        reduced[i, pl.ds(0, BLK), :] = dot(place, hub_grads[...]).astype(BF)


def local(
    features,
    hub_features,
    hub_order,
    tile_values,
    tile_dest,
    tile_source,
    tile_count,
    self_weight,
    neighbour_weight,
    cotangent,
):
    rows, width = features.shape
    window = {o: to_region(features, -o[0], o[1]) for o in OTHERS}
    hubs = spread(spread(hub_features, WIDE, N_WIDE), NEAR, N_NEAR)
    side = lax.axis_index("yl").astype(jnp.int32).reshape(1)
    smem = pl.BlockSpec(memory_space=pltpu.SMEM)
    vmem = pl.BlockSpec(memory_space=pltpu.VMEM)
    hbm = pl.BlockSpec(memory_space=pl.ANY)
    shape = jax.ShapeDtypeStruct
    wide = shape((rows, width), BF)
    outs = pl.pallas_call(
        kernel,
        in_specs=[smem] * 4 + [hbm] * 6 + [vmem] * 7,
        out_specs=[vmem] * 8,
        out_shape=[wide, shape((rows, width), F32)] + [wide] * 5 + [shape((N_NEAR, 2 * BLK, width), BF)],
        scratch_shapes=[
            pltpu.VMEM((4, 8 * BLK, width), BF),
            pltpu.VMEM((4, 4, BLK, width), F32),
            pltpu.VMEM((4, 8 * BLK, width), F32),
            pltpu.VMEM((rows, width), BF),
            pltpu.VMEM((rows, width), BF),
            pltpu.VMEM((rows, width), BF),
            pltpu.VMEM((8 * BLK, width), BF),
            pltpu.SemaphoreType.DMA((6,)),
        ],
        compiler_params=pltpu.CompilerParams(vmem_limit_bytes=52 * 1024 * 1024),
        cost_estimate=pl.CostEstimate(flops=4 * 10**9, bytes_accessed=14 * 10**6, transcendentals=0),
    )(
        tile_dest, tile_source, tile_count, side,
        features, *(window[o] for o in OTHERS),
        hubs, hub_order.reshape(-1, 1), hub_order.reshape(1, -1), tile_values,
        self_weight, neighbour_weight, cotangent,
    )
    embedding, own_grad, sent, reduced = outs[0], outs[1], outs[2:7], outs[7]
    back = [to_region(g, o[0], o[1]) for g, o in zip(sent, OTHERS)]
    part = collect(reduced, NEAR).astype(BF)
    hub_part, weight_part = part[:BLK], part[BLK:]
    part = jnp.concatenate([hub_part.reshape(N_WIDE, 4, width), weight_part.reshape(N_WIDE, 4, width)], 1)
    part = collect(part, WIDE)
    hub_gradient = part[:4]
    weights = spread(spread(part[4:].astype(BF), WIDE, N_WIDE), NEAR, N_NEAR).astype(F32)
    feature_gradient = own_grad
    for g in back:
        feature_gradient = feature_gradient + g.astype(F32)
    return embedding, feature_gradient, hub_gradient, weights[:width], weights[width:]


def solution(mesh):
    fine = Mesh(mesh.devices.reshape(EXTENT), AXES)
    split = P(AXES)
    in_specs = (split, split, P(), split, split, split, split, P(), P(), split)
    out_specs = (split, split, split, P(), P())
    return jax.shard_map(local, mesh=fine, in_specs=in_specs, out_specs=out_specs, check_vma=False)
```

```python
import functools

import jax
import jax.numpy as jnp
from jax import lax
from jax.experimental import pallas as pl
from jax.experimental.pallas import tpu as pltpu
from jax.sharding import Mesh
from jax.sharding import PartitionSpec as P

BF = jnp.bfloat16
F32 = jnp.float32
BLK = 128
AXES = ("x", "z", "yh", "core", "yl")
EXTENT = (4, 8, 2, 2, 2)
WIDE = ("z", "yh", "yl")
N_WIDE, N_X = 32, 4
DEVICES = 256


def to_core(value):
    return lax.ppermute(value, AXES, [(d, d ^ 2) for d in range(DEVICES)])


def to_side(value):
    return lax.ppermute(value, AXES, [(d, d ^ 1) for d in range(DEVICES)])


def to_off(value):
    pairs = []
    for d in range(DEVICES):
        region = d // 2
        other = region + (1 if region % 2 else -1)
        if 0 <= other < DEVICES // 2:
            pairs.append((d, 2 * other + (1 - d % 2)))
    return lax.ppermute(value, AXES, pairs)


def spread(value, axes, count):
    copies = jnp.broadcast_to(value[None], (count,) + value.shape)
    return lax.all_to_all(copies, axes, 0, 0, tiled=True).reshape(-1, value.shape[-1])


def to_x(value, flip):
    return lax.ppermute(value, "x", [(x, x ^ flip) for x in range(N_X)])


def collect_x(parts):
    total = parts[0].astype(F32)
    for j in range(1, N_X):
        total = total + to_x(parts[j], j).astype(F32)
    return total.astype(BF)


def hub_of(position):
    low = position & 7
    core = (position >> 7) & 1
    mid = (position >> 3) & 15
    high = position >> 8
    return low | (core << 3) | (mid << 4) | (high << 8)


def dot(a, b, ca=1, cb=0):
    return lax.dot_general(a, b, (((ca,), (cb,)), ((), ())), preferred_element_type=F32)


def prepare(order_col, order_row, core, x_ref, features, self_weight, pick, place, own_pre):
    for r in range(2):
        for x in range(N_X):
            here = pl.ds(x * BLK, BLK)
            ids = hub_of(lax.broadcasted_iota(jnp.int32, (BLK, BLK), 1) + (2 * x + (core[0] ^ r)) * BLK)
            there = (2 * (x_ref[0] ^ x) + (core[0] ^ r)) * BLK
            back = hub_of(lax.broadcasted_iota(jnp.int32, (BLK, BLK), 0) + there)
            for j in range(8):
                rows = pl.ds(j * BLK, BLK)
                pick[r, rows, here] = (order_col[rows, :] == ids).astype(F32).astype(BF)
                place[r, here, rows] = (back == order_row[:, rows]).astype(F32).astype(BF)
    for b in range(4):
        rows = pl.ds(b * BLK, BLK)
        own_pre[rows, :] = dot(features[rows, :], self_weight[...])


LOW = (16, 0, 8, 24)


def slot(dest, source, live, flip, m, cat):
    k = 4 * m + cat
    block = source[0, k] - LOW[cat]
    if cat < 3:
        block = block ^ flip
    mask = jnp.where(k < live, 1.0, 0.0).astype(BF)
    return k, dest[0, k], pl.ds(pl.multiple_of(block * BLK, BLK), BLK), mask


def put(r, j, keep, send, value):
    if r == 0:
        keep[j][...] = value.astype(BF)
    else:
        send[pl.ds(j * BLK, BLK), :] = value.astype(BF)


def ahead(
    dest, source, count, side, core_ref, x_ref,
    features, own_other, on_same, on_other, off_same_low, off_same_high, off_other,
    hubs_hbm, hubs_there_hbm, pick_hbm, own_pre_hbm, tiles_hbm, neigh_weight_hbm, cotangent_hbm,
    embedding, slope, *rest,
):
    keep, send = rest[:N_X], rest[N_X]
    table, sums, left, hubs, hubs_there, pick, own_pre, tiles, neigh_weight, cotangent, sems = rest[N_X + 1:]
    live = count[0]
    flip = 4 * side[0]
    core = core_ref[0]
    def load(n, source_ref, target):
        copy = pltpu.make_async_copy(source_ref, target, sems.at[n])
        copy.start()
        return copy

    first = [
        load(n, *refs)
        for n, refs in enumerate(((hubs_hbm, hubs), (hubs_there_hbm, hubs_there), (pick_hbm, pick)))
    ]
    second = [load(3, tiles_hbm, tiles)]
    for n, (ref, cat, block) in enumerate((
        (on_same, core, 0), (on_other, core, 4), (off_same_low, 1 - core, 0), (off_same_high, 1 - core, 2),
        (off_other, 1 - core, 4), (features, 2, 0), (own_other, 2, 4),
    )):
        second.append(load(4 + n, ref, table.at[cat, pl.ds(block * BLK, ref.shape[0])]))
    third = [
        load(11 + n, *refs)
        for n, refs in enumerate(((own_pre_hbm, own_pre), (neigh_weight_hbm, neigh_weight), (cotangent_hbm, cotangent)))
    ]
    sums[...] = jnp.zeros_like(sums)
    for copy in first:
        copy.wait()
    for j in range(8):
        rows = pl.ds(j * BLK, BLK)
        table[3, rows, :] = (dot(pick[0, rows, :], hubs[...]) + dot(pick[1, rows, :], hubs_there[...])).astype(BF)
    for copy in second:
        copy.wait()

    def forward(m, carry):
        for cat in range(4):
            k, d, rows, mask = slot(dest, source, live, flip, m, cat)
            sums[cat, d] += dot(tiles[k] * mask, table[cat, rows, :])
        return carry

    lax.fori_loop(0, (live + 3) // 4, forward, 0)
    for copy in third:
        copy.wait()

    for b in range(4):
        rows = pl.ds(b * BLK, BLK)
        near = (sums[0, b] + sums[1, b] + sums[2, b] + sums[3, b]).astype(BF)
        left[0, rows, :] = table[2, rows, :]
        left[1, rows, :] = near
        pre = own_pre[rows, :] + dot(near, neigh_weight[...])
        sig = jax.nn.sigmoid(pre)
        embedding[rows, :] = (pre * sig).astype(BF)
        slope[rows, :] = (cotangent[rows, :].astype(F32) * (sig * (1.0 + pre * (1.0 - sig)))).astype(BF)
    for r in range(2):
        for j in range(N_X):
            x = x_ref[0] ^ j
            first = (2 * (x & 1) + (core ^ r)) * BLK
            columns = pl.ds(pl.multiple_of(first, BLK), BLK)
            put(r, j, keep, send, dot(left[x >> 1, :, columns], slope[...], 0, 0))


def behind(
    dest, source, count, side, core_ref,
    slope, place, tiles, self_weight, neigh_weight,
    own_grad, g_own_other, g_on_same, g_on_other, g_off_same, g_off_other, *rest,
):
    keep, send, (grads, back, hub_grads) = rest[:N_X], rest[N_X], rest[N_X + 1:]
    live = count[0]
    flip = 4 * side[0]
    core = core_ref[0]
    grads[...] = jnp.zeros_like(grads)
    for b in range(4):
        rows = pl.ds(b * BLK, BLK)
        back[rows, :] = dot(slope[rows, :], neigh_weight[...], 1, 1).astype(BF)
        own_grad[rows, :] = dot(slope[rows, :], self_weight[...], 1, 1)

    def backward(m, carry):
        for cat in range(4):
            k, d, rows, mask = slot(dest, source, live, flip, m, cat)
            there = pl.ds(pl.multiple_of(d * BLK, BLK), BLK)
            grads[cat, rows, :] += dot(tiles[k] * mask, back[there, :], 0, 0)
        return carry

    lax.fori_loop(0, (live + 3) // 4, backward, 0)
    half, rest = pl.ds(0, 4 * BLK), pl.ds(4 * BLK, 4 * BLK)
    g_on_same[...] = grads[core, half, :].astype(BF)
    g_on_other[...] = grads[core, rest, :].astype(BF)
    g_off_same[...] = grads[1 - core, half, :].astype(BF)
    g_off_other[...] = grads[1 - core, rest, :].astype(BF)
    g_own_other[...] = grads[2, rest, :].astype(BF)
    own_grad[...] += grads[2, half, :]
    hub_grads[...] = grads[3].astype(BF)
    for r in range(2):
        for j in range(N_X):
            put(r, j, keep, send, dot(place[r, pl.ds(j * BLK, BLK), :], hub_grads[...]))


def join_cores(parts):
    theirs = to_core(parts[-1])
    return [plus(mine, theirs[j * BLK:(j + 1) * BLK]) for j, mine in enumerate(parts[:-1])]


def plus(a, b):
    return (a.astype(F32) + b.astype(F32)).astype(BF)


def local(
    features,
    hub_features,
    hub_order,
    tile_values,
    tile_dest,
    tile_source,
    tile_count,
    self_weight,
    neighbour_weight,
    cotangent,
):
    rows, width = features.shape
    smem = pl.BlockSpec(memory_space=pltpu.SMEM)
    vmem = pl.BlockSpec(memory_space=pltpu.VMEM)
    hbm = pl.BlockSpec(memory_space=pl.ANY)
    shape = jax.ShapeDtypeStruct
    wide = shape((rows, width), BF)
    part = shape((BLK, width), BF)
    params = pltpu.CompilerParams(vmem_limit_bytes=56 * 1024 * 1024)
    side = lax.axis_index("yl").astype(jnp.int32).reshape(1)
    core = lax.axis_index("core").astype(jnp.int32).reshape(1)
    x = lax.axis_index("x").astype(jnp.int32).reshape(1)
    where = (tile_dest, tile_source, tile_count, side, core)
    barrier = lax.optimization_barrier

    own_other = to_side(features)
    off_other = to_off(features)
    on_same = to_core(features)
    hubs = spread(hub_features, WIDE, N_WIDE)
    pick, place, own_pre = pl.pallas_call(
        prepare,
        in_specs=[vmem, vmem, smem, smem, vmem, vmem],
        out_specs=[vmem] * 3,
        out_shape=[
            shape((2, 8 * BLK, 4 * BLK), BF),
            shape((2, 4 * BLK, 8 * BLK), BF),
            shape((rows, width), F32),
        ],
        compiler_params=params,
        cost_estimate=pl.CostEstimate(flops=3 * 10**8, bytes_accessed=6 * 10**6, transcendentals=0),
        name="prepare",
    )(hub_order.reshape(-1, 1), hub_order.reshape(1, -1), core, x, features, self_weight)
    own_other, off_other, on_same, hubs, pick, place, own_pre = barrier(
        (own_other, off_other, on_same, hubs, pick, place, own_pre)
    )
    off_same_low = to_side(off_other[:rows // 2])
    off_same_high = to_off(own_other[rows // 2:])
    on_other = to_core(own_other)
    hubs = spread(hubs, ("x",), N_X)
    hubs, off_same_low, off_same_high, on_other = barrier((hubs, off_same_low, off_same_high, on_other))
    hubs_there = to_core(hubs)

    embedding, slope, *w = pl.pallas_call(
        ahead,
        in_specs=[smem] * 6 + [hbm] * 14,
        out_specs=[vmem] * (3 + N_X),
        out_shape=[wide, wide] + [part] * N_X + [wide],
        scratch_shapes=[
            pltpu.VMEM((4, 8 * BLK, width), BF),
            pltpu.VMEM((4, 4, BLK, width), F32),
            pltpu.VMEM((2, rows, width), BF),
            pltpu.VMEM((4 * BLK, width), BF),
            pltpu.VMEM((4 * BLK, width), BF),
            pltpu.VMEM((2, 8 * BLK, 4 * BLK), BF),
            pltpu.VMEM((rows, width), F32),
            pltpu.VMEM(tile_values.shape, BF),
            pltpu.VMEM((width, width), BF),
            pltpu.VMEM((rows, width), BF),
            pltpu.SemaphoreType.DMA((14,)),
        ],
        compiler_params=params,
        cost_estimate=pl.CostEstimate(flops=2 * 10**9, bytes_accessed=10 * 10**6, transcendentals=0),
        name="ahead",
    )(
        *where, x,
        features, own_other, on_same, on_other, off_same_low, off_same_high, off_other,
        hubs, hubs_there, pick, own_pre, tile_values, neighbour_weight, cotangent,
    )
    w = join_cores(w)
    w, slope = barrier((w, slope))

    own_grad, g_own_other, g_on_same, g_on_other, g_off_same, g_off_other, *h = pl.pallas_call(
        behind,
        in_specs=[smem] * 5 + [vmem] * 5,
        out_specs=[vmem] * (7 + N_X),
        out_shape=[shape((rows, width), F32)] + [wide] * 5 + [part] * N_X + [wide],
        scratch_shapes=[
            pltpu.VMEM((4, 8 * BLK, width), F32),
            pltpu.VMEM((rows, width), BF),
            pltpu.VMEM((8 * BLK, width), BF),
        ],
        compiler_params=params,
        cost_estimate=pl.CostEstimate(flops=2 * 10**9, bytes_accessed=10 * 10**6, transcendentals=0),
        name="behind",
    )(*where, slope, place, tile_values, self_weight, neighbour_weight)

    w = collect_x(w)
    g = (g_own_other, g_on_same, g_on_other, g_off_same, g_off_other)
    w, h, g = barrier((w, h, g))
    g_own_other, g_on_same, g_on_other, g_off_same, g_off_other = g
    w, h = barrier((w, join_cores(h)))

    w = lax.all_to_all(w.reshape(N_WIDE, 4, width), WIDE, 0, 0, tiled=True).astype(F32).sum(0).astype(BF)
    h = collect_x(h)
    r_on_other = to_core(g_on_other)
    r_off_same = to_side(g_off_same)
    r_on_same = to_core(g_on_same)
    s_side = plus(g_own_other, r_on_other)
    s_off = plus(g_off_other, r_off_same)

    w, h, s_side, s_off, r_on_same = barrier((w, h, s_side, s_off, r_on_same))
    r_side = to_side(s_side)
    r_off = to_off(s_off)
    both = jnp.concatenate([jnp.broadcast_to(w[None], (N_WIDE, 4, width)), h.reshape(N_WIDE, 4, width)], 1)
    both = lax.all_to_all(both, WIDE, 0, 0, tiled=True)
    w = both[:, :4].reshape(BLK, width)
    hub_gradient = both[:, 4:].astype(F32).sum(0)
    w = spread(w, ("x",), N_X)
    w, r_side, r_off = barrier((w, r_side, r_off))
    there = to_core(w)
    feature_gradient = own_grad + r_on_same.astype(F32) + r_side.astype(F32) + r_off.astype(F32)
    first = core[0] == 0
    pair = (N_X, 1, BLK, width)
    low, high = jnp.where(first, w, there).reshape(pair), jnp.where(first, there, w).reshape(pair)
    weights = jnp.concatenate([low, high], 1).reshape(2, width, width).astype(F32)
    return embedding, feature_gradient, hub_gradient, weights[0], weights[1]


def solution(mesh):
    fine = Mesh(mesh.devices.reshape(EXTENT), AXES)
    split = P(AXES)
    in_specs = (split, split, P(), split, split, split, split, P(), P(), split)
    out_specs = (split, split, split, P(), P())
    return jax.shard_map(local, mesh=fine, in_specs=in_specs, out_specs=out_specs, check_vma=False)
```

```python
import functools

import jax
import jax.numpy as jnp
from jax import lax
from jax.experimental import pallas as pl
from jax.experimental.pallas import tpu as pltpu
from jax.sharding import Mesh
from jax.sharding import PartitionSpec as P

BF = jnp.bfloat16
F32 = jnp.float32
BLK = 128
AXES = ("x", "z", "yh", "core", "yl")
EXTENT = (4, 8, 2, 2, 2)
WIDE = ("z", "yh", "yl")
N_WIDE, N_X = 32, 4
DEVICES = 256


def to_core(value):
    return lax.ppermute(value, AXES, [(d, d ^ 2) for d in range(DEVICES)])


def to_side(value):
    return lax.ppermute(value, AXES, [(d, d ^ 1) for d in range(DEVICES)])


def to_off(value):
    pairs = []
    for d in range(DEVICES):
        region = d // 2
        other = region + (1 if region % 2 else -1)
        if 0 <= other < DEVICES // 2:
            pairs.append((d, 2 * other + (1 - d % 2)))
    return lax.ppermute(value, AXES, pairs)


def spread(value, axes, count):
    copies = jnp.broadcast_to(value[None], (count,) + value.shape)
    return lax.all_to_all(copies, axes, 0, 0, tiled=True).reshape(-1, value.shape[-1])


def to_x(value, flip):
    return lax.ppermute(value, "x", [(x, x ^ flip) for x in range(N_X)])


def collect_x(parts):
    total = parts[0].astype(F32)
    for j in range(1, N_X):
        total = total + to_x(parts[j], j).astype(F32)
    return total.astype(BF)


def hub_of(position):
    low = position & 7
    core = (position >> 7) & 1
    mid = (position >> 3) & 15
    high = position >> 8
    return low | (core << 3) | (mid << 4) | (high << 8)


def dot(a, b, ca=1, cb=0):
    return lax.dot_general(a, b, (((ca,), (cb,)), ((), ())), preferred_element_type=F32)


def prepare(
    dest, source, count, side, core_ref, order_col, features_hbm, self_weight_hbm, tiles_hbm,
    near, own_pre,
    cells, hub_cells, pick, features, self_weight, tiles, sems,
):
    copies = [
        pltpu.make_async_copy(*refs, sems.at[n])
        for n, refs in enumerate(((tiles_hbm, tiles), (features_hbm, features), (self_weight_hbm, self_weight)))
    ]
    for copy in copies:
        copy.start()
    live, flip, core = count[0], 4 * side[0], core_ref[0]
    for r in range(2):
        for x in range(N_X):
            ids = hub_of(lax.broadcasted_iota(jnp.int32, (BLK, BLK), 1) + (2 * x + (core ^ r)) * BLK)
            for j in range(8):
                rows = pl.ds(j * BLK, BLK)
                pick[r, rows, pl.ds(x * BLK, BLK)] = (order_col[rows, :] == ids).astype(F32).astype(BF)
    cells[...] = jnp.zeros_like(cells)
    for copy in copies:
        copy.wait()
    low = (16, 0, 8, 24)
    base = (2 + 2 * core, 4 - 2 * core, 0, 6)

    def add(m, carry):
        for cat in range(4):
            k = 4 * m + cat
            block = source[0, k] - low[cat]
            if cat < 3:
                block = block ^ flip
            rows = pl.ds(pl.multiple_of(dest[0, k] * BLK, BLK), BLK)
            cells[base[cat] + (block >> 2), block & 3, rows, :] += jnp.where(k < live, tiles[k].astype(F32), 0.0)
        return carry

    lax.fori_loop(0, (live + 3) // 4, add, 0)
    for p in range(8):
        for j in range(4):
            cell = cells[p, j].astype(BF)
            if p < 6:
                near[p, :, pl.ds(j * BLK, BLK)] = cell
            else:
                hub_cells[:, pl.ds(((p - 6) * 4 + j) * BLK, BLK)] = cell
    for r in range(2):
        near[6 + r] = dot(hub_cells[...], pick[r]).astype(BF)
    own_pre[...] = dot(features[...], self_weight[...])


def put(r, j, keep, send, value):
    if r == 0:
        keep[j][...] = value.astype(BF)
    else:
        send[pl.ds(j * BLK, BLK), :] = value.astype(BF)


def ahead(
    core_ref, x_ref, near_hbm,
    features, own_other, on_same, on_other, off_same_low, off_same_high, off_other, hubs, hubs_there,
    own_pre_hbm, neigh_weight_hbm, cotangent_hbm,
    embedding, slope, *rest,
):
    keep, send = rest[:N_X], rest[N_X]
    near, table, sums, left, own_pre, neigh_weight, cotangent, sems = rest[N_X + 1:]
    core = core_ref[0]
    half = 2 * BLK

    def load(n, source_ref, target):
        copy = pltpu.make_async_copy(source_ref, target, sems.at[n])
        copy.start()
        return copy

    waits = []
    n = 0
    for p, refs in enumerate((
        (features,), (own_other,), (on_same,), (on_other,), (off_same_low, off_same_high), (off_other,),
        (hubs,), (hubs_there,),
    )):
        waits.append([load(n, near_hbm.at[p], near.at[p])])
        n += 1
        for i, ref in enumerate(refs):
            waits[-1].append(load(n, ref, table.at[p, pl.ds(i * half, ref.shape[0])]))
            n += 1
    last = [
        load(n + i, *refs)
        for i, refs in enumerate(((own_pre_hbm, own_pre), (neigh_weight_hbm, neigh_weight), (cotangent_hbm, cotangent)))
    ]
    for p in range(8):
        for copy in waits[p]:
            copy.wait()
        value = dot(near[p], table[p])
        sums[...] = value if p == 0 else sums[...] + value
    for copy in last:
        copy.wait()
    left[0] = table[0]
    for b in range(4):
        rows = pl.ds(b * BLK, BLK)
        aggregate = sums[rows, :].astype(BF)
        left[1, rows, :] = aggregate
        pre = own_pre[rows, :] + dot(aggregate, neigh_weight[...])
        sig = jax.nn.sigmoid(pre)
        embedding[rows, :] = (pre * sig).astype(BF)
        slope[rows, :] = (cotangent[rows, :].astype(F32) * (sig * (1.0 + pre * (1.0 - sig)))).astype(BF)
    for r in range(2):
        for j in range(N_X):
            x = x_ref[0] ^ j
            first = (2 * (x & 1) + (core ^ r)) * BLK
            columns = pl.ds(pl.multiple_of(first, BLK), BLK)
            put(r, j, keep, send, dot(left[x >> 1, :, columns], slope[...], 0, 0))


def behind(
    x_ref, near_hbm, slope_hbm, self_weight_hbm, neigh_weight_hbm,
    own_grad, g_own_other, g_on_same, g_on_other, g_off_same, g_off_other, *rest,
):
    keep, send = rest[:N_X], rest[N_X]
    near, back, slope, self_weight, neigh_weight, sems = rest[N_X + 1:]
    first = [
        pltpu.make_async_copy(*refs, sems.at[n])
        for n, refs in enumerate((
            (slope_hbm, slope), (neigh_weight_hbm, neigh_weight), (self_weight_hbm, self_weight),
        ))
    ]
    order = (6, 7, 1, 2, 3, 4, 5, 0)
    second = [pltpu.make_async_copy(near_hbm.at[p], near.at[p], sems.at[3 + p]) for p in range(8)]
    for copy in first + [second[p] for p in order]:
        copy.start()
    for copy in first:
        copy.wait()
    back[...] = dot(slope[...], neigh_weight[...], 1, 1).astype(BF)
    outs = (None, g_own_other, g_on_same, g_on_other, g_off_same, g_off_other)
    for p in order:
        second[p].wait()
        if p >= 6:
            for j in range(N_X):
                columns = pl.ds(pl.multiple_of((x_ref[0] ^ j) * BLK, BLK), BLK)
                put(p - 6, j, keep, send, dot(near[p, :, columns], back[...], 0, 0))
        elif p > 0:
            outs[p][...] = dot(near[p], back[...], 0, 0).astype(BF)
        else:
            own_grad[...] = dot(near[p], back[...], 0, 0) + dot(slope[...], self_weight[...], 1, 1)


def join_cores(parts):
    theirs = to_core(parts[-1])
    return [plus(mine, theirs[j * BLK:(j + 1) * BLK]) for j, mine in enumerate(parts[:-1])]


def plus(a, b):
    return (a.astype(F32) + b.astype(F32)).astype(BF)


def local(
    features,
    hub_features,
    hub_order,
    tile_values,
    tile_dest,
    tile_source,
    tile_count,
    self_weight,
    neighbour_weight,
    cotangent,
):
    rows, width = features.shape
    smem = pl.BlockSpec(memory_space=pltpu.SMEM)
    vmem = pl.BlockSpec(memory_space=pltpu.VMEM)
    hbm = pl.BlockSpec(memory_space=pl.ANY)
    shape = jax.ShapeDtypeStruct
    wide = shape((rows, width), BF)
    part = shape((BLK, width), BF)
    params = pltpu.CompilerParams(vmem_limit_bytes=56 * 1024 * 1024)
    side = lax.axis_index("yl").astype(jnp.int32).reshape(1)
    core = lax.axis_index("core").astype(jnp.int32).reshape(1)
    x = lax.axis_index("x").astype(jnp.int32).reshape(1)
    barrier = lax.optimization_barrier

    own_other = to_side(features)
    off_other = to_off(features)
    on_same = to_core(features)
    hubs = spread(hub_features, WIDE, N_WIDE)
    pieces = shape((8, rows, width), BF)
    near, own_pre = pl.pallas_call(
        prepare,
        in_specs=[smem] * 5 + [vmem] + [hbm] * 3,
        out_specs=[vmem] * 2,
        out_shape=[pieces, shape((rows, width), F32)],
        scratch_shapes=[
            pltpu.VMEM((8, 4, rows, BLK), F32),
            pltpu.VMEM((rows, 8 * BLK), BF),
            pltpu.VMEM((2, 8 * BLK, 4 * BLK), BF),
            pltpu.VMEM((rows, width), BF),
            pltpu.VMEM((width, width), BF),
            pltpu.VMEM(tile_values.shape, BF),
            pltpu.SemaphoreType.DMA((3,)),
        ],
        compiler_params=params,
        cost_estimate=pl.CostEstimate(flops=13 * 10**8, bytes_accessed=9 * 10**6, transcendentals=0),
        name="prepare",
    )(tile_dest, tile_source, tile_count, side, core, hub_order.reshape(-1, 1), features, self_weight, tile_values)
    own_other, off_other, on_same, hubs, near, own_pre = barrier((own_other, off_other, on_same, hubs, near, own_pre))
    off_same_low = to_side(off_other[:rows // 2])
    off_same_high = to_off(own_other[rows // 2:])
    on_other = to_core(own_other)
    hubs = spread(hubs, ("x",), N_X)
    hubs, off_same_low, off_same_high, on_other = barrier((hubs, off_same_low, off_same_high, on_other))
    hubs_there = to_core(hubs)

    embedding, slope, *w = pl.pallas_call(
        ahead,
        in_specs=[smem] * 2 + [hbm] * 13,
        out_specs=[vmem] * (3 + N_X),
        out_shape=[wide, wide] + [part] * N_X + [wide],
        scratch_shapes=[
            pltpu.VMEM((8, rows, width), BF),
            pltpu.VMEM((8, rows, width), BF),
            pltpu.VMEM((rows, width), F32),
            pltpu.VMEM((2, rows, width), BF),
            pltpu.VMEM((rows, width), F32),
            pltpu.VMEM((width, width), BF),
            pltpu.VMEM((rows, width), BF),
            pltpu.SemaphoreType.DMA((20,)),
        ],
        compiler_params=params,
        cost_estimate=pl.CostEstimate(flops=3 * 10**9, bytes_accessed=12 * 10**6, transcendentals=0),
        name="ahead",
    )(
        core, x, near,
        features, own_other, on_same, on_other, off_same_low, off_same_high, off_other, hubs, hubs_there,
        own_pre, neighbour_weight, cotangent,
    )
    w = join_cores(w)
    w, slope = barrier((w, slope))

    own_grad, g_own_other, g_on_same, g_on_other, g_off_same, g_off_other, *h = pl.pallas_call(
        behind,
        in_specs=[smem] + [hbm] * 4,
        out_specs=[vmem] * (7 + N_X),
        out_shape=[shape((rows, width), F32)] + [wide] * 5 + [part] * N_X + [wide],
        scratch_shapes=[
            pltpu.VMEM((8, rows, width), BF),
            pltpu.VMEM((rows, width), BF),
            pltpu.VMEM((rows, width), BF),
            pltpu.VMEM((width, width), BF),
            pltpu.VMEM((width, width), BF),
            pltpu.SemaphoreType.DMA((11,)),
        ],
        compiler_params=params,
        cost_estimate=pl.CostEstimate(flops=3 * 10**9, bytes_accessed=10 * 10**6, transcendentals=0),
        name="behind",
    )(x, near, slope, self_weight, neighbour_weight)

    w = collect_x(w)
    g = (g_own_other, g_on_same, g_on_other, g_off_same, g_off_other)
    w, h, g = barrier((w, h, g))
    g_own_other, g_on_same, g_on_other, g_off_same, g_off_other = g
    w, h = barrier((w, join_cores(h)))

    w = lax.all_to_all(w.reshape(N_WIDE, 4, width), WIDE, 0, 0, tiled=True).astype(F32).sum(0).astype(BF)
    h = collect_x(h)
    r_on_other = to_core(g_on_other)
    r_off_same = to_side(g_off_same)
    r_on_same = to_core(g_on_same)
    s_side = plus(g_own_other, r_on_other)
    s_off = plus(g_off_other, r_off_same)

    w, h, s_side, s_off, r_on_same = barrier((w, h, s_side, s_off, r_on_same))
    r_side = to_side(s_side)
    r_off = to_off(s_off)
    both = jnp.concatenate([jnp.broadcast_to(w[None], (N_WIDE, 4, width)), h.reshape(N_WIDE, 4, width)], 1)
    both = lax.all_to_all(both, WIDE, 0, 0, tiled=True)
    w = both[:, :4].reshape(BLK, width)
    hub_gradient = both[:, 4:].astype(F32).sum(0)
    w = spread(w, ("x",), N_X)
    w, r_side, r_off = barrier((w, r_side, r_off))
    there = to_core(w)
    feature_gradient = own_grad + r_on_same.astype(F32) + r_side.astype(F32) + r_off.astype(F32)
    first = core[0] == 0
    pair = (N_X, 1, BLK, width)
    low, high = jnp.where(first, w, there).reshape(pair), jnp.where(first, there, w).reshape(pair)
    weights = jnp.concatenate([low, high], 1).reshape(2, width, width).astype(F32)
    return embedding, feature_gradient, hub_gradient, weights[0], weights[1]


def solution(mesh):
    fine = Mesh(mesh.devices.reshape(EXTENT), AXES)
    split = P(AXES)
    in_specs = (split, split, P(), split, split, split, split, P(), P(), split)
    out_specs = (split, split, split, P(), P())
    return jax.shard_map(local, mesh=fine, in_specs=in_specs, out_specs=out_specs, check_vma=False)
```

```python
import functools

import jax
import jax.numpy as jnp
from jax import lax
from jax.experimental import pallas as pl
from jax.experimental.pallas import tpu as pltpu
from jax.sharding import Mesh
from jax.sharding import PartitionSpec as P

BF = jnp.bfloat16
F32 = jnp.float32
BLK = 128
AXES = ("x", "z", "yh", "core", "yl")
EXTENT = (4, 8, 2, 2, 2)
WIDE = ("z", "yh", "yl")
N_WIDE, N_X = 32, 4
DEVICES = 256


def to_core(value):
    return lax.ppermute(value, AXES, [(d, d ^ 2) for d in range(DEVICES)])


def to_side(value):
    return lax.ppermute(value, AXES, [(d, d ^ 1) for d in range(DEVICES)])


def to_off(value):
    pairs = []
    for d in range(DEVICES):
        region = d // 2
        other = region + (1 if region % 2 else -1)
        if 0 <= other < DEVICES // 2:
            pairs.append((d, 2 * other + (1 - d % 2)))
    return lax.ppermute(value, AXES, pairs)


def spread(value, axes, count):
    copies = jnp.broadcast_to(value[None], (count,) + value.shape)
    return lax.all_to_all(copies, axes, 0, 0, tiled=True).reshape(-1, value.shape[-1])


def to_x(value, flip):
    return lax.ppermute(value, "x", [(x, x ^ flip) for x in range(N_X)])


def collect_x(parts):
    total = parts[0].astype(F32)
    for j in range(1, N_X):
        total = total + to_x(parts[j], j).astype(F32)
    return total.astype(BF)


def hub_of(position):
    low = position & 7
    core = (position >> 7) & 1
    mid = (position >> 3) & 15
    high = position >> 8
    return low | (core << 3) | (mid << 4) | (high << 8)


def dot(a, b, ca=1, cb=0):
    return lax.dot_general(a, b, (((ca,), (cb,)), ((), ())), preferred_element_type=F32)


def prepare(
    dest, source, count, side, core_ref, order_col, features_hbm, self_weight_hbm, tiles_hbm,
    near, own_pre,
    cells, hub_cells, pick, features, self_weight, tiles, sems,
):
    copies = [
        pltpu.make_async_copy(*refs, sems.at[n])
        for n, refs in enumerate(((tiles_hbm, tiles), (features_hbm, features), (self_weight_hbm, self_weight)))
    ]
    for copy in copies:
        copy.start()
    live, flip, core = count[0], 4 * side[0], core_ref[0]
    for r in range(2):
        for x in range(N_X):
            ids = hub_of(lax.broadcasted_iota(jnp.int32, (BLK, BLK), 1) + (2 * x + (core ^ r)) * BLK)
            for j in range(8):
                rows = pl.ds(j * BLK, BLK)
                pick[r, rows, pl.ds(x * BLK, BLK)] = (order_col[rows, :] == ids).astype(F32).astype(BF)
    cells[...] = jnp.zeros_like(cells)
    for copy in copies:
        copy.wait()
    low = (16, 0, 8, 24)
    base = (2 + 2 * core, 4 - 2 * core, 0, 6)

    def add(m, carry):
        for cat in range(4):
            k = 4 * m + cat
            block = source[0, k] - low[cat]
            if cat < 3:
                block = block ^ flip
            rows = pl.ds(pl.multiple_of(dest[0, k] * BLK, BLK), BLK)
            cells[base[cat] + (block >> 2), block & 3, rows, :] += jnp.where(k < live, tiles[k].astype(F32), 0.0)
        return carry

    lax.fori_loop(0, (live + 3) // 4, add, 0)
    for p in range(8):
        for j in range(4):
            cell = cells[p, j].astype(BF)
            if p < 6:
                near[p, :, pl.ds(j * BLK, BLK)] = cell
            else:
                hub_cells[:, pl.ds(((p - 6) * 4 + j) * BLK, BLK)] = cell
    for r in range(2):
        near[6 + r] = dot(hub_cells[...], pick[r]).astype(BF)
    own_pre[...] = dot(features[...], self_weight[...])


def ahead(
    core_ref, x_ref, near_hbm,
    features, own_other, on_same, on_other, off_same_low, off_same_high, off_other, hubs, hubs_there,
    own_pre_hbm, neigh_weight_hbm, cotangent_hbm,
    embedding, slope, back, send, *rest,
):
    keep, keep_hub = rest[:N_X], rest[N_X:2 * N_X]
    near, table, sums, left, own_pre, neigh_weight, cotangent, sems = rest[2 * N_X:]
    core = core_ref[0]
    half = 2 * BLK

    def load(n, source_ref, target):
        copy = pltpu.make_async_copy(source_ref, target, sems.at[n])
        copy.start()
        return copy

    waits = []
    n = 0
    for p, refs in enumerate((
        (features,), (own_other,), (on_same,), (on_other,), (off_same_low, off_same_high), (off_other,),
        (hubs,), (hubs_there,),
    )):
        waits.append([load(n, near_hbm.at[p], near.at[p])])
        n += 1
        for i, ref in enumerate(refs):
            waits[-1].append(load(n, ref, table.at[p, pl.ds(i * half, ref.shape[0])]))
            n += 1
    last = [
        load(n + i, *refs)
        for i, refs in enumerate(((own_pre_hbm, own_pre), (neigh_weight_hbm, neigh_weight), (cotangent_hbm, cotangent)))
    ]
    for p in range(8):
        for copy in waits[p]:
            copy.wait()
        value = dot(near[p], table[p])
        sums[...] = value if p == 0 else sums[...] + value
    for copy in last:
        copy.wait()
    left[0] = table[0]
    for b in range(4):
        rows = pl.ds(b * BLK, BLK)
        aggregate = sums[rows, :].astype(BF)
        left[1, rows, :] = aggregate
        pre = own_pre[rows, :] + dot(aggregate, neigh_weight[...])
        sig = jax.nn.sigmoid(pre)
        embedding[rows, :] = (pre * sig).astype(BF)
        slope[rows, :] = (cotangent[rows, :].astype(F32) * (sig * (1.0 + pre * (1.0 - sig)))).astype(BF)
    back[...] = dot(slope[...], neigh_weight[...], 1, 1).astype(BF)
    for r in range(2):
        for j in range(N_X):
            x = x_ref[0] ^ j
            first = (2 * (x & 1) + (core ^ r)) * BLK
            columns = pl.ds(pl.multiple_of(first, BLK), BLK)
            value = dot(left[x >> 1, :, columns], slope[...], 0, 0).astype(BF)
            columns = pl.ds(pl.multiple_of(x * BLK, BLK), BLK)
            hub_value = dot(near[6 + r, :, columns], back[...], 0, 0).astype(BF)
            if r == 0:
                keep[j][...] = value
                keep_hub[j][...] = hub_value
            else:
                send[pl.ds(j * BLK, BLK), :] = value
                send[pl.ds((N_X + j) * BLK, BLK), :] = hub_value


def behind(
    near_hbm, back_hbm, slope_hbm, self_weight_hbm,
    own_grad, g_own_other, g_on_same, g_on_other, g_off_same, g_off_other,
    near, back, slope, self_weight, sems,
):
    order = (1, 2, 3, 4, 5, 0)
    moves = [(back_hbm, back)] + [(near_hbm.at[p], near.at[p]) for p in order]
    moves += [(slope_hbm, slope), (self_weight_hbm, self_weight)]
    copies = [pltpu.make_async_copy(*refs, sems.at[n]) for n, refs in enumerate(moves)]
    for copy in copies:
        copy.start()
    copies[0].wait()
    outs = (None, g_own_other, g_on_same, g_on_other, g_off_same, g_off_other)
    for n, p in enumerate(order[:-1]):
        copies[1 + n].wait()
        outs[p][...] = dot(near[p], back[...], 0, 0).astype(BF)
    for copy in copies[6:]:
        copy.wait()
    own_grad[...] = dot(near[0], back[...], 0, 0) + dot(slope[...], self_weight[...], 1, 1)


def plus(a, b):
    return (a.astype(F32) + b.astype(F32)).astype(BF)


def local(
    features,
    hub_features,
    hub_order,
    tile_values,
    tile_dest,
    tile_source,
    tile_count,
    self_weight,
    neighbour_weight,
    cotangent,
):
    rows, width = features.shape
    smem = pl.BlockSpec(memory_space=pltpu.SMEM)
    vmem = pl.BlockSpec(memory_space=pltpu.VMEM)
    hbm = pl.BlockSpec(memory_space=pl.ANY)
    shape = jax.ShapeDtypeStruct
    wide = shape((rows, width), BF)
    part = shape((BLK, width), BF)
    params = pltpu.CompilerParams(vmem_limit_bytes=56 * 1024 * 1024)
    side = lax.axis_index("yl").astype(jnp.int32).reshape(1)
    core = lax.axis_index("core").astype(jnp.int32).reshape(1)
    x = lax.axis_index("x").astype(jnp.int32).reshape(1)
    barrier = lax.optimization_barrier

    own_other = to_side(features)
    off_other = to_off(features)
    on_same = to_core(features)
    hubs = spread(hub_features, WIDE, N_WIDE)
    pieces = shape((8, rows, width), BF)
    near, own_pre = pl.pallas_call(
        prepare,
        in_specs=[smem] * 5 + [vmem] + [hbm] * 3,
        out_specs=[vmem] * 2,
        out_shape=[pieces, shape((rows, width), F32)],
        scratch_shapes=[
            pltpu.VMEM((8, 4, rows, BLK), F32),
            pltpu.VMEM((rows, 8 * BLK), BF),
            pltpu.VMEM((2, 8 * BLK, 4 * BLK), BF),
            pltpu.VMEM((rows, width), BF),
            pltpu.VMEM((width, width), BF),
            pltpu.VMEM(tile_values.shape, BF),
            pltpu.SemaphoreType.DMA((3,)),
        ],
        compiler_params=params,
        cost_estimate=pl.CostEstimate(flops=13 * 10**8, bytes_accessed=9 * 10**6, transcendentals=0),
        name="prepare",
    )(tile_dest, tile_source, tile_count, side, core, hub_order.reshape(-1, 1), features, self_weight, tile_values)
    own_other, off_other, on_same, hubs, near, own_pre = barrier((own_other, off_other, on_same, hubs, near, own_pre))
    off_same_low = to_side(off_other[:rows // 2])
    off_same_high = to_off(own_other[rows // 2:])
    on_other = to_core(own_other)
    hubs = spread(hubs, ("x",), N_X)
    hubs, off_same_low, off_same_high, on_other = barrier((hubs, off_same_low, off_same_high, on_other))
    hubs_there = to_core(hubs)

    embedding, slope, back, send, *kept = pl.pallas_call(
        ahead,
        in_specs=[smem] * 2 + [hbm] * 13,
        out_specs=[vmem] * (4 + 2 * N_X),
        out_shape=[wide] * 3 + [shape((2 * rows, width), BF)] + [part] * (2 * N_X),
        scratch_shapes=[
            pltpu.VMEM((8, rows, width), BF),
            pltpu.VMEM((8, rows, width), BF),
            pltpu.VMEM((rows, width), F32),
            pltpu.VMEM((2, rows, width), BF),
            pltpu.VMEM((rows, width), F32),
            pltpu.VMEM((width, width), BF),
            pltpu.VMEM((rows, width), BF),
            pltpu.SemaphoreType.DMA((20,)),
        ],
        compiler_params=params,
        cost_estimate=pl.CostEstimate(flops=4 * 10**9, bytes_accessed=12 * 10**6, transcendentals=0),
        name="ahead",
    )(
        core, x, near,
        features, own_other, on_same, on_other, off_same_low, off_same_high, off_other, hubs, hubs_there,
        own_pre, neighbour_weight, cotangent,
    )
    theirs = to_core(send)
    kept = [plus(mine, theirs[j * BLK:(j + 1) * BLK]) for j, mine in enumerate(kept)]
    w, h = kept[:N_X], kept[N_X:]
    w, h, slope, back = barrier((w, h, slope, back))

    own_grad, g_own_other, g_on_same, g_on_other, g_off_same, g_off_other = pl.pallas_call(
        behind,
        in_specs=[hbm] * 4,
        out_specs=[vmem] * 6,
        out_shape=[shape((rows, width), F32)] + [wide] * 5,
        scratch_shapes=[
            pltpu.VMEM((8, rows, width), BF),
            pltpu.VMEM((rows, width), BF),
            pltpu.VMEM((rows, width), BF),
            pltpu.VMEM((width, width), BF),
            pltpu.SemaphoreType.DMA((9,)),
        ],
        compiler_params=params,
        cost_estimate=pl.CostEstimate(flops=2 * 10**9, bytes_accessed=8 * 10**6, transcendentals=0),
        name="behind",
    )(near, back, slope, self_weight)

    w = collect_x(w)
    g = (g_own_other, g_on_same, g_on_other, g_off_same, g_off_other)
    w, h, g = barrier((w, h, g))
    g_own_other, g_on_same, g_on_other, g_off_same, g_off_other = g
    w = lax.all_to_all(w.reshape(N_WIDE, 4, width), WIDE, 0, 0, tiled=True).astype(F32).sum(0).astype(BF)
    h = collect_x(h)
    r_on_other = to_core(g_on_other)
    r_off_same = to_side(g_off_same)
    r_on_same = to_core(g_on_same)

    w, h, r_on_other, r_off_same, r_on_same = barrier((w, h, r_on_other, r_off_same, r_on_same))
    s_side = plus(g_own_other, r_on_other)
    s_off = plus(g_off_other, r_off_same)
    r_side = to_side(s_side)
    r_off = to_off(s_off)
    both = jnp.concatenate([jnp.broadcast_to(w[None], (N_WIDE, 4, width)), h.reshape(N_WIDE, 4, width)], 1)
    both = lax.all_to_all(both, WIDE, 0, 0, tiled=True)
    w = both[:, :4].reshape(BLK, width)
    hub_gradient = both[:, 4:].astype(F32).sum(0)
    w = spread(w, ("x",), N_X)
    w, r_side, r_off = barrier((w, r_side, r_off))
    there = to_core(w)
    feature_gradient = own_grad + r_on_same.astype(F32) + r_side.astype(F32) + r_off.astype(F32)
    mine = lax.broadcasted_iota(jnp.int32, (1, 2, 1, 1), 1) == core[0]
    w, there = w.reshape(N_X, 1, BLK, width), there.reshape(N_X, 1, BLK, width)
    weights = [
        jnp.where(mine, w[i:i + 2], there[i:i + 2]).astype(F32).reshape(width, width) for i in (0, 2)
    ]
    return embedding, feature_gradient, hub_gradient, weights[0], weights[1]


def solution(mesh):
    fine = Mesh(mesh.devices.reshape(EXTENT), AXES)
    split = P(AXES)
    in_specs = (split, split, P(), split, split, split, split, P(), P(), split)
    out_specs = (split, split, split, P(), P())
    return jax.shard_map(local, mesh=fine, in_specs=in_specs, out_specs=out_specs, check_vma=False)
```

```python
import functools

import jax
import jax.numpy as jnp
from jax import lax
from jax.experimental import pallas as pl
from jax.experimental.pallas import tpu as pltpu
from jax.sharding import Mesh
from jax.sharding import PartitionSpec as P

BF = jnp.bfloat16
F32 = jnp.float32
BLK = 128
AXES = ("x", "z", "yh", "core", "yl")
EXTENT = (4, 8, 2, 2, 2)
WIDE = ("z", "yh", "yl")
N_WIDE, N_X = 32, 4
DEVICES = 256


def to_core(value):
    return lax.ppermute(value, AXES, [(d, d ^ 2) for d in range(DEVICES)])


def to_side(value):
    return lax.ppermute(value, AXES, [(d, d ^ 1) for d in range(DEVICES)])


def to_off(value):
    pairs = []
    for d in range(DEVICES):
        region = d // 2
        other = region + (1 if region % 2 else -1)
        if 0 <= other < DEVICES // 2:
            pairs.append((d, 2 * other + (1 - d % 2)))
    return lax.ppermute(value, AXES, pairs)


def spread(value, axes, count):
    copies = jnp.broadcast_to(value[None], (count,) + value.shape)
    return lax.all_to_all(copies, axes, 0, 0, tiled=True).reshape(-1, value.shape[-1])


def to_x(value, flip):
    return lax.ppermute(value, "x", [(x, x ^ flip) for x in range(N_X)])


def collect_x(parts):
    total = parts[0].astype(F32)
    for j in range(1, N_X):
        total = total + to_x(parts[j], j).astype(F32)
    return total.astype(BF)


def hub_of(position):
    low = position & 7
    core = (position >> 7) & 1
    mid = (position >> 3) & 15
    high = position >> 8
    return low | (core << 3) | (mid << 4) | (high << 8)


def dot(a, b, ca=1, cb=0):
    return lax.dot_general(a, b, (((ca,), (cb,)), ((), ())), preferred_element_type=F32)


def prepare(
    dest, source, count, side, core_ref, order_col, features_hbm, self_weight_hbm, tiles_hbm,
    near, own_pre,
    cells, hub_cells, pick, features, self_weight, tiles, sems,
):
    copies = [
        pltpu.make_async_copy(*refs, sems.at[n])
        for n, refs in enumerate(((tiles_hbm, tiles), (features_hbm, features), (self_weight_hbm, self_weight)))
    ]
    for copy in copies:
        copy.start()
    live, flip, core = count[0], 4 * side[0], core_ref[0]
    for r in range(2):
        for x in range(N_X):
            ids = hub_of(lax.broadcasted_iota(jnp.int32, (BLK, BLK), 1) + (2 * x + (core ^ r)) * BLK)
            for j in range(8):
                rows = pl.ds(j * BLK, BLK)
                pick[r, rows, pl.ds(x * BLK, BLK)] = (order_col[rows, :] == ids).astype(F32).astype(BF)
    cells[...] = jnp.zeros_like(cells)
    for copy in copies:
        copy.wait()
    low = (16, 0, 8, 24)
    base = (2 + 2 * core, 4 - 2 * core, 0, 6)

    def add(m, carry):
        for cat in range(4):
            k = 4 * m + cat
            block = source[0, k] - low[cat]
            if cat < 3:
                block = block ^ flip
            rows = pl.ds(pl.multiple_of(dest[0, k] * BLK, BLK), BLK)
            cells[base[cat] + (block >> 2), block & 3, rows, :] += jnp.where(k < live, tiles[k].astype(F32), 0.0)
        return carry

    lax.fori_loop(0, (live + 3) // 4, add, 0)
    for p in range(8):
        for j in range(4):
            cell = cells[p, j].astype(BF)
            if p < 6:
                near[p, :, pl.ds(j * BLK, BLK)] = cell
            else:
                hub_cells[:, pl.ds(((p - 6) * 4 + j) * BLK, BLK)] = cell
    for r in range(2):
        near[6 + r] = dot(hub_cells[...], pick[r]).astype(BF)
    own_pre[...] = dot(features[...], self_weight[...])


def ahead(
    core_ref, x_ref, near_hbm,
    features, own_other, on_same, on_other, off_same_low, off_same_high, off_other, hubs, hubs_there,
    own_pre_hbm, neigh_weight_hbm, cotangent_hbm,
    embedding, slope, back, send, *rest,
):
    keep, keep_hub = rest[:N_X], rest[N_X:2 * N_X]
    near, table, sums, left, own_pre, neigh_weight, cotangent, sems = rest[2 * N_X:]
    core = core_ref[0]
    half = 2 * BLK

    def load(n, source_ref, target):
        copy = pltpu.make_async_copy(source_ref, target, sems.at[n])
        copy.start()
        return copy

    waits = []
    n = 0
    for p, refs in enumerate((
        (features,), (own_other,), (on_same,), (on_other,), (off_same_low, off_same_high), (off_other,),
        (hubs,), (hubs_there,),
    )):
        waits.append([load(n, near_hbm.at[p], near.at[p])])
        n += 1
        for i, ref in enumerate(refs):
            waits[-1].append(load(n, ref, table.at[p, pl.ds(i * half, ref.shape[0])]))
            n += 1
    last = [
        load(n + i, *refs)
        for i, refs in enumerate(((own_pre_hbm, own_pre), (neigh_weight_hbm, neigh_weight), (cotangent_hbm, cotangent)))
    ]
    for p in range(8):
        for copy in waits[p]:
            copy.wait()
        value = dot(near[p], table[p])
        sums[...] = value if p == 0 else sums[...] + value
    for copy in last:
        copy.wait()
    left[0] = table[0]
    for b in range(4):
        rows = pl.ds(b * BLK, BLK)
        aggregate = sums[rows, :].astype(BF)
        left[1, rows, :] = aggregate
        pre = own_pre[rows, :] + dot(aggregate, neigh_weight[...])
        sig = jax.nn.sigmoid(pre)
        embedding[rows, :] = (pre * sig).astype(BF)
        slope[rows, :] = (cotangent[rows, :].astype(F32) * (sig * (1.0 + pre * (1.0 - sig)))).astype(BF)
    back[...] = dot(slope[...], neigh_weight[...], 1, 1).astype(BF)
    for r in range(2):
        for j in range(N_X):
            x = x_ref[0] ^ j
            first = (2 * (x & 1) + (core ^ r)) * BLK
            columns = pl.ds(pl.multiple_of(first, BLK), BLK)
            value = dot(left[x >> 1, :, columns], slope[...], 0, 0).astype(BF)
            columns = pl.ds(pl.multiple_of(x * BLK, BLK), BLK)
            hub_value = dot(near[6 + r, :, columns], back[...], 0, 0).astype(BF)
            if r == 0:
                keep[j][...] = value
                keep_hub[j][...] = hub_value
            else:
                send[pl.ds(j * BLK, BLK), :] = value
                send[pl.ds((N_X + j) * BLK, BLK), :] = hub_value


def behind(
    near_hbm, back_hbm, slope_hbm, self_weight_hbm,
    own_grad, g_own_other, g_on, g_off_same, g_off_other,
    near, back, slope, self_weight, sems,
):
    order = (1, 2, 3, 4, 5, 0)
    moves = [(back_hbm, back)] + [(near_hbm.at[p], near.at[p]) for p in order]
    moves += [(slope_hbm, slope), (self_weight_hbm, self_weight)]
    copies = [pltpu.make_async_copy(*refs, sems.at[n]) for n, refs in enumerate(moves)]
    for copy in copies:
        copy.start()
    copies[0].wait()
    rows = near.shape[1]
    outs = (None, g_own_other, g_on.at[pl.ds(0, rows)], g_on.at[pl.ds(rows, rows)], g_off_same, g_off_other)
    for n, p in enumerate(order[:-1]):
        copies[1 + n].wait()
        outs[p][...] = dot(near[p], back[...], 0, 0).astype(BF)
    for copy in copies[6:]:
        copy.wait()
    own_grad[...] = dot(near[0], back[...], 0, 0) + dot(slope[...], self_weight[...], 1, 1)


def plus(a, b):
    return (a.astype(F32) + b.astype(F32)).astype(BF)


def local(
    features,
    hub_features,
    hub_order,
    tile_values,
    tile_dest,
    tile_source,
    tile_count,
    self_weight,
    neighbour_weight,
    cotangent,
):
    rows, width = features.shape
    smem = pl.BlockSpec(memory_space=pltpu.SMEM)
    vmem = pl.BlockSpec(memory_space=pltpu.VMEM)
    hbm = pl.BlockSpec(memory_space=pl.ANY)
    shape = jax.ShapeDtypeStruct
    wide = shape((rows, width), BF)
    part = shape((BLK, width), BF)
    params = pltpu.CompilerParams(vmem_limit_bytes=56 * 1024 * 1024)
    side = lax.axis_index("yl").astype(jnp.int32).reshape(1)
    core = lax.axis_index("core").astype(jnp.int32).reshape(1)
    x = lax.axis_index("x").astype(jnp.int32).reshape(1)
    barrier = lax.optimization_barrier

    own_other = to_side(features)
    off_other = to_off(features)
    on_same = to_core(features)
    hubs = spread(hub_features, WIDE, N_WIDE)
    pieces = shape((8, rows, width), BF)
    near, own_pre = pl.pallas_call(
        prepare,
        in_specs=[smem] * 5 + [vmem] + [hbm] * 3,
        out_specs=[vmem] * 2,
        out_shape=[pieces, shape((rows, width), F32)],
        scratch_shapes=[
            pltpu.VMEM((8, 4, rows, BLK), F32),
            pltpu.VMEM((rows, 8 * BLK), BF),
            pltpu.VMEM((2, 8 * BLK, 4 * BLK), BF),
            pltpu.VMEM((rows, width), BF),
            pltpu.VMEM((width, width), BF),
            pltpu.VMEM(tile_values.shape, BF),
            pltpu.SemaphoreType.DMA((3,)),
        ],
        compiler_params=params,
        cost_estimate=pl.CostEstimate(flops=13 * 10**8, bytes_accessed=9 * 10**6, transcendentals=0),
        name="prepare",
    )(tile_dest, tile_source, tile_count, side, core, hub_order.reshape(-1, 1), features, self_weight, tile_values)
    own_other, off_other, on_same, hubs, near, own_pre = barrier((own_other, off_other, on_same, hubs, near, own_pre))
    off_same_low = to_side(off_other[:rows // 2])
    off_same_high = to_off(own_other[rows // 2:])
    on_other = to_core(own_other)
    hubs = spread(hubs, ("x",), N_X)
    hubs, off_same_low, off_same_high, on_other = barrier((hubs, off_same_low, off_same_high, on_other))
    hubs_there = to_core(hubs)

    embedding, slope, back, send, *kept = pl.pallas_call(
        ahead,
        in_specs=[smem] * 2 + [hbm] * 13,
        out_specs=[vmem] * (4 + 2 * N_X),
        out_shape=[wide] * 3 + [shape((2 * rows, width), BF)] + [part] * (2 * N_X),
        scratch_shapes=[
            pltpu.VMEM((8, rows, width), BF),
            pltpu.VMEM((8, rows, width), BF),
            pltpu.VMEM((rows, width), F32),
            pltpu.VMEM((2, rows, width), BF),
            pltpu.VMEM((rows, width), F32),
            pltpu.VMEM((width, width), BF),
            pltpu.VMEM((rows, width), BF),
            pltpu.SemaphoreType.DMA((20,)),
        ],
        compiler_params=params,
        cost_estimate=pl.CostEstimate(flops=4 * 10**9, bytes_accessed=12 * 10**6, transcendentals=0),
        name="ahead",
    )(
        core, x, near,
        features, own_other, on_same, on_other, off_same_low, off_same_high, off_other, hubs, hubs_there,
        own_pre, neighbour_weight, cotangent,
    )
    theirs = to_core(send)
    kept = [plus(mine, theirs[j * BLK:(j + 1) * BLK]) for j, mine in enumerate(kept)]
    w, h = kept[:N_X], kept[N_X:]
    w, h, slope, back = barrier((w, h, slope, back))

    own_grad, g_own_other, g_on, g_off_same, g_off_other = pl.pallas_call(
        behind,
        in_specs=[hbm] * 4,
        out_specs=[vmem] * 5,
        out_shape=[shape((rows, width), F32), wide, shape((2 * rows, width), BF), wide, wide],
        scratch_shapes=[
            pltpu.VMEM((8, rows, width), BF),
            pltpu.VMEM((rows, width), BF),
            pltpu.VMEM((rows, width), BF),
            pltpu.VMEM((width, width), BF),
            pltpu.SemaphoreType.DMA((9,)),
        ],
        compiler_params=params,
        cost_estimate=pl.CostEstimate(flops=2 * 10**9, bytes_accessed=8 * 10**6, transcendentals=0),
        name="behind",
    )(near, back, slope, self_weight)

    w = collect_x(w)
    g = (g_own_other, g_on, g_off_same, g_off_other)
    w, h, g = barrier((w, h, g))
    g_own_other, g_on, g_off_same, g_off_other = g
    w = lax.all_to_all(w.reshape(N_WIDE, 4, width), WIDE, 0, 0, tiled=True).astype(F32).sum(0).astype(BF)
    h = collect_x(h)
    r_on = to_core(g_on)
    r_off_same = to_side(g_off_same)

    w, h, r_on, r_off_same = barrier((w, h, r_on, r_off_same))
    s_side = plus(g_own_other, r_on[rows:])
    s_off = plus(g_off_other, r_off_same)
    r_side = to_side(s_side)
    r_off = to_off(s_off)
    both = jnp.concatenate([jnp.broadcast_to(w[None], (N_WIDE, 4, width)), h.reshape(N_WIDE, 4, width)], 1)
    both = lax.all_to_all(both, WIDE, 0, 0, tiled=True)
    w = both[:, :4].reshape(BLK, width)
    hub_gradient = both[:, 4:].astype(F32).sum(0)
    w = spread(w, ("x",), N_X)
    w, r_side, r_off = barrier((w, r_side, r_off))
    there = to_core(w)
    feature_gradient = own_grad + r_on[:rows].astype(F32) + r_side.astype(F32) + r_off.astype(F32)
    mine = lax.broadcasted_iota(jnp.int32, (1, 2, 1, 1), 1) == core[0]
    w, there = w.reshape(N_X, 1, BLK, width), there.reshape(N_X, 1, BLK, width)
    weights = [
        jnp.where(mine, w[i:i + 2], there[i:i + 2]).astype(F32).reshape(width, width) for i in (0, 2)
    ]
    return embedding, feature_gradient, hub_gradient, weights[0], weights[1]


def solution(mesh):
    fine = Mesh(mesh.devices.reshape(EXTENT), AXES)
    split = P(AXES)
    in_specs = (split, split, P(), split, split, split, split, P(), P(), split)
    out_specs = (split, split, split, P(), P())
    return jax.shard_map(local, mesh=fine, in_specs=in_specs, out_specs=out_specs, check_vma=False)
```

```python
import functools

import jax
import jax.numpy as jnp
from jax import lax
from jax.experimental import pallas as pl
from jax.experimental.pallas import tpu as pltpu
from jax.sharding import Mesh
from jax.sharding import PartitionSpec as P

BF = jnp.bfloat16
F32 = jnp.float32
BLK = 128
AXES = ("x", "z", "yh", "core", "yl")
EXTENT = (4, 8, 2, 2, 2)
WIDE = ("z", "yh", "yl")
N_WIDE, N_X = 32, 4
DEVICES = 256


def to_core(value):
    return lax.ppermute(value, AXES, [(d, d ^ 2) for d in range(DEVICES)])


def to_side(value):
    return lax.ppermute(value, AXES, [(d, d ^ 1) for d in range(DEVICES)])


def to_off(value):
    pairs = []
    for d in range(DEVICES):
        region = d // 2
        other = region + (1 if region % 2 else -1)
        if 0 <= other < DEVICES // 2:
            pairs.append((d, 2 * other + (1 - d % 2)))
    return lax.ppermute(value, AXES, pairs)


def spread(value, axes, count):
    copies = jnp.broadcast_to(value[None], (count,) + value.shape)
    return lax.all_to_all(copies, axes, 0, 0, tiled=True).reshape(-1, value.shape[-1])


def to_x(value, flip):
    return lax.ppermute(value, "x", [(x, x ^ flip) for x in range(N_X)])


def collect_x(parts):
    total = parts[0].astype(F32)
    for j in range(1, N_X):
        total = total + to_x(parts[j], j).astype(F32)
    return total.astype(BF)


def hub_of(position):
    low = position & 7
    core = (position >> 7) & 1
    mid = (position >> 3) & 15
    high = position >> 8
    return low | (core << 3) | (mid << 4) | (high << 8)


def dot(a, b, ca=1, cb=0):
    return lax.dot_general(a, b, (((ca,), (cb,)), ((), ())), preferred_element_type=F32)


def prepare(
    dest, source, count, side, core_ref, order, features_hbm, self_weight_hbm, tiles_hbm,
    near_hbm, own_pre,
    near, cells, hub_cells, place, features, self_weight, tiles, sems,
):
    copies = [
        pltpu.make_async_copy(*refs, sems.at[n])
        for n, refs in enumerate(((tiles_hbm, tiles), (features_hbm, features), (self_weight_hbm, self_weight)))
    ]
    for copy in copies:
        copy.start()
    live, flip, core = count[0], 4 * side[0], core_ref[0]
    for r in range(2):
        for x in range(N_X):
            ids = hub_of(lax.broadcasted_iota(jnp.int32, (BLK, BLK), 0) + (2 * x + (core ^ r)) * BLK)
            for j in range(8):
                columns = pl.ds(j * BLK, BLK)
                place[r, pl.ds(x * BLK, BLK), columns] = (ids == order[:, columns]).astype(F32).astype(BF)
    cells[...] = jnp.zeros_like(cells)
    for copy in copies:
        copy.wait()
    low = (16, 0, 8, 24)
    base = (2 + 2 * core, 4 - 2 * core, 0, 6)

    def add(m, carry):
        for cat in range(4):
            k = 4 * m + cat
            block = source[0, k] - low[cat]
            if cat < 3:
                block = block ^ flip
            rows = pl.ds(pl.multiple_of(dest[0, k] * BLK, BLK), BLK)
            cells[base[cat] + (block >> 2), block & 3, rows, :] += jnp.where(k < live, tiles[k].astype(F32), 0.0)
        return carry

    lax.fori_loop(0, (live + 3) // 4, add, 0)
    stores = [pltpu.make_async_copy(near.at[p], near_hbm.at[p], sems.at[3 + p]) for p in range(8)]
    for j in range(8):
        hub_cells[:, pl.ds(j * BLK, BLK)] = cells[6 + j // 4, j % 4].astype(BF)
    for r in range(2):
        near[6 + r] = dot(hub_cells[...], place[r], 1, 1).astype(BF)
        stores[6 + r].start()
    for p in range(6):
        for j in range(4):
            near[p, :, pl.ds(j * BLK, BLK)] = cells[p, j].astype(BF)
        stores[p].start()
    own_pre[...] = dot(features[...], self_weight[...])
    for store in stores:
        store.wait()


def ahead(
    core_ref, x_ref, near_hbm,
    features, own_other, on_same, on_other, off_same_low, off_same_high, off_other, hubs, hubs_there,
    own_pre_hbm, neigh_weight_hbm, cotangent_hbm,
    embedding, slope, back, send, *rest,
):
    keep, keep_hub = rest[:N_X], rest[N_X:2 * N_X]
    near, table, sums, left, own_pre, neigh_weight, cotangent, sems = rest[2 * N_X:]
    core = core_ref[0]
    half = 2 * BLK

    def load(n, source_ref, target):
        copy = pltpu.make_async_copy(source_ref, target, sems.at[n])
        copy.start()
        return copy

    waits = []
    n = 0
    for p, refs in enumerate((
        (features,), (own_other,), (on_same,), (on_other,), (off_same_low, off_same_high), (off_other,),
        (hubs,), (hubs_there,),
    )):
        waits.append([load(n, near_hbm.at[p], near.at[p])])
        n += 1
        for i, ref in enumerate(refs):
            waits[-1].append(load(n, ref, table.at[p, pl.ds(i * half, ref.shape[0])]))
            n += 1
    last = [
        load(n + i, *refs)
        for i, refs in enumerate(((own_pre_hbm, own_pre), (neigh_weight_hbm, neigh_weight), (cotangent_hbm, cotangent)))
    ]
    for p in range(8):
        for copy in waits[p]:
            copy.wait()
        value = dot(near[p], table[p])
        sums[...] = value if p == 0 else sums[...] + value
    for copy in last:
        copy.wait()
    left[0] = table[0]
    for b in range(4):
        rows = pl.ds(b * BLK, BLK)
        aggregate = sums[rows, :].astype(BF)
        left[1, rows, :] = aggregate
        pre = own_pre[rows, :] + dot(aggregate, neigh_weight[...])
        sig = jax.nn.sigmoid(pre)
        embedding[rows, :] = (pre * sig).astype(BF)
        slope[rows, :] = (cotangent[rows, :].astype(F32) * (sig * (1.0 + pre * (1.0 - sig)))).astype(BF)
    back[...] = dot(slope[...], neigh_weight[...], 1, 1).astype(BF)
    for r in range(2):
        for j in range(N_X):
            x = x_ref[0] ^ j
            first = (2 * (x & 1) + (core ^ r)) * BLK
            columns = pl.ds(pl.multiple_of(first, BLK), BLK)
            value = dot(left[x >> 1, :, columns], slope[...], 0, 0).astype(BF)
            columns = pl.ds(pl.multiple_of(x * BLK, BLK), BLK)
            hub_value = dot(near[6 + r, :, columns], back[...], 0, 0).astype(BF)
            if r == 0:
                keep[j][...] = value
                keep_hub[j][...] = hub_value
            else:
                send[pl.ds(j * BLK, BLK), :] = value
                send[pl.ds((N_X + j) * BLK, BLK), :] = hub_value


def behind(
    near_hbm, back_hbm, slope_hbm, self_weight_hbm,
    own_grad, g_own_other, g_on, g_off_same, g_off_other,
    near, back, slope, self_weight, sems,
):
    order = (1, 2, 3, 4, 5, 0)
    moves = [(back_hbm, back)] + [(near_hbm.at[p], near.at[p]) for p in order]
    moves += [(slope_hbm, slope), (self_weight_hbm, self_weight)]
    copies = [pltpu.make_async_copy(*refs, sems.at[n]) for n, refs in enumerate(moves)]
    for copy in copies:
        copy.start()
    copies[0].wait()
    rows = near.shape[1]
    outs = (None, g_own_other, g_on.at[pl.ds(0, rows)], g_on.at[pl.ds(rows, rows)], g_off_same, g_off_other)
    for n, p in enumerate(order[:-1]):
        copies[1 + n].wait()
        outs[p][...] = dot(near[p], back[...], 0, 0).astype(BF)
    for copy in copies[6:]:
        copy.wait()
    own_grad[...] = dot(near[0], back[...], 0, 0) + dot(slope[...], self_weight[...], 1, 1)


def plus(a, b):
    return (a.astype(F32) + b.astype(F32)).astype(BF)


def local(
    features,
    hub_features,
    hub_order,
    tile_values,
    tile_dest,
    tile_source,
    tile_count,
    self_weight,
    neighbour_weight,
    cotangent,
):
    rows, width = features.shape
    smem = pl.BlockSpec(memory_space=pltpu.SMEM)
    vmem = pl.BlockSpec(memory_space=pltpu.VMEM)
    hbm = pl.BlockSpec(memory_space=pl.ANY)
    shape = jax.ShapeDtypeStruct
    wide = shape((rows, width), BF)
    part = shape((BLK, width), BF)
    params = pltpu.CompilerParams(vmem_limit_bytes=56 * 1024 * 1024)
    side = lax.axis_index("yl").astype(jnp.int32).reshape(1)
    core = lax.axis_index("core").astype(jnp.int32).reshape(1)
    x = lax.axis_index("x").astype(jnp.int32).reshape(1)
    barrier = lax.optimization_barrier

    own_other = to_side(features)
    off_other = to_off(features)
    hubs = spread(hub_features, WIDE, N_WIDE)
    pieces = shape((8, rows, width), BF)
    near, own_pre = pl.pallas_call(
        prepare,
        in_specs=[smem] * 5 + [vmem] + [hbm] * 3,
        out_specs=[hbm, vmem],
        out_shape=[pieces, shape((rows, width), F32)],
        scratch_shapes=[
            pltpu.VMEM((8, rows, width), BF),
            pltpu.VMEM((8, 4, rows, BLK), F32),
            pltpu.VMEM((rows, 8 * BLK), BF),
            pltpu.VMEM((2, 4 * BLK, 8 * BLK), BF),
            pltpu.VMEM((rows, width), BF),
            pltpu.VMEM((width, width), BF),
            pltpu.VMEM(tile_values.shape, BF),
            pltpu.SemaphoreType.DMA((11,)),
        ],
        compiler_params=params,
        cost_estimate=pl.CostEstimate(flops=13 * 10**8, bytes_accessed=9 * 10**6, transcendentals=0),
        name="prepare",
    )(tile_dest, tile_source, tile_count, side, core, hub_order.reshape(1, -1), features, self_weight, tile_values)
    own_other, off_other, hubs, near, own_pre, rows_here = barrier((own_other, off_other, hubs, near, own_pre, features))
    on_same = to_core(rows_here)
    off_same_low = to_side(off_other[:rows // 2])
    off_same_high = to_off(own_other[rows // 2:])
    on_other = to_core(own_other)
    hubs = spread(hubs, ("x",), N_X)
    hubs, off_same_low, off_same_high, on_same, on_other = barrier(
        (hubs, off_same_low, off_same_high, on_same, on_other)
    )
    hubs_there = to_core(hubs)

    embedding, slope, back, send, *kept = pl.pallas_call(
        ahead,
        in_specs=[smem] * 2 + [hbm] * 13,
        out_specs=[vmem] * (4 + 2 * N_X),
        out_shape=[wide] * 3 + [shape((2 * rows, width), BF)] + [part] * (2 * N_X),
        scratch_shapes=[
            pltpu.VMEM((8, rows, width), BF),
            pltpu.VMEM((8, rows, width), BF),
            pltpu.VMEM((rows, width), F32),
            pltpu.VMEM((2, rows, width), BF),
            pltpu.VMEM((rows, width), F32),
            pltpu.VMEM((width, width), BF),
            pltpu.VMEM((rows, width), BF),
            pltpu.SemaphoreType.DMA((20,)),
        ],
        compiler_params=params,
        cost_estimate=pl.CostEstimate(flops=4 * 10**9, bytes_accessed=12 * 10**6, transcendentals=0),
        name="ahead",
    )(
        core, x, near,
        features, own_other, on_same, on_other, off_same_low, off_same_high, off_other, hubs, hubs_there,
        own_pre, neighbour_weight, cotangent,
    )
    theirs = to_core(send)
    kept = [plus(mine, theirs[j * BLK:(j + 1) * BLK]) for j, mine in enumerate(kept)]
    w, h = kept[:N_X], kept[N_X:]
    w, h, slope, back = barrier((w, h, slope, back))

    own_grad, g_own_other, g_on, g_off_same, g_off_other = pl.pallas_call(
        behind,
        in_specs=[hbm] * 4,
        out_specs=[vmem] * 5,
        out_shape=[shape((rows, width), F32), wide, shape((2 * rows, width), BF), wide, wide],
        scratch_shapes=[
            pltpu.VMEM((8, rows, width), BF),
            pltpu.VMEM((rows, width), BF),
            pltpu.VMEM((rows, width), BF),
            pltpu.VMEM((width, width), BF),
            pltpu.SemaphoreType.DMA((9,)),
        ],
        compiler_params=params,
        cost_estimate=pl.CostEstimate(flops=2 * 10**9, bytes_accessed=8 * 10**6, transcendentals=0),
        name="behind",
    )(near, back, slope, self_weight)

    w = collect_x(w)
    g = (g_own_other, g_on, g_off_same, g_off_other)
    w, h, g = barrier((w, h, g))
    g_own_other, g_on, g_off_same, g_off_other = g
    w = lax.all_to_all(w.reshape(N_WIDE, 4, width), WIDE, 0, 0, tiled=True).astype(F32).sum(0).astype(BF)
    h = collect_x(h)
    r_on = to_core(g_on)
    r_off_same = to_side(g_off_same)

    w, h, r_on, r_off_same = barrier((w, h, r_on, r_off_same))
    s_side = plus(g_own_other, r_on[rows:])
    s_off = plus(g_off_other, r_off_same)
    r_side = to_side(s_side)
    r_off = to_off(s_off)
    both = jnp.concatenate([jnp.broadcast_to(w[None], (N_WIDE, 4, width)), h.reshape(N_WIDE, 4, width)], 1)
    both = lax.all_to_all(both, WIDE, 0, 0, tiled=True)
    w = both[:, :4].reshape(BLK, width)
    hub_gradient = both[:, 4:].astype(F32).sum(0)
    w = spread(w, ("x",), N_X)
    w, r_side, r_off = barrier((w, r_side, r_off))
    there = to_core(w)
    feature_gradient = own_grad + r_on[:rows].astype(F32) + r_side.astype(F32) + r_off.astype(F32)
    mine = lax.broadcasted_iota(jnp.int32, (1, 2, 1, 1), 1) == core[0]
    w, there = w.reshape(N_X, 1, BLK, width), there.reshape(N_X, 1, BLK, width)
    weights = [
        jnp.where(mine, w[i:i + 2], there[i:i + 2]).astype(F32).reshape(width, width) for i in (0, 2)
    ]
    return embedding, feature_gradient, hub_gradient, weights[0], weights[1]


def solution(mesh):
    fine = Mesh(mesh.devices.reshape(EXTENT), AXES)
    split = P(AXES)
    in_specs = (split, split, P(), split, split, split, split, P(), P(), split)
    out_specs = (split, split, split, P(), P())
    return jax.shard_map(local, mesh=fine, in_specs=in_specs, out_specs=out_specs, check_vma=False)
```
